256 devices in a mesh: ctx: 32 (over y_lo, z, core), head: 8 (over y_hi, x).
Axes of the slice: x: 4, y: 4 (y_hi: 2, y_lo: 2; y = y_hi * 2 + y_lo), z: 8, core: 2. Of those that a mesh axis runs over, the one named last changes fastest.
Arguments:
- q_nope: bfloat16 [8192, 128, 128], P('ctx', 'head'), may hold values from -6 to 6
- q_rope: bfloat16 [8192, 8192], P('ctx', 'head'), may hold values from -400 to 400
- latent: bfloat16 [8192, 576], P('ctx'), may hold values from -8 to 8
- w_uk: bfloat16 [512, 128, 128], P(None, 'head'), may hold values from -0.25 to 0.25
- w_uv: bfloat16 [512, 128, 128], P(None, 'head'), may hold values from -0.25 to 0.25
- span_order: int32 [64], replicated, may hold values from 0 to 63, each once
Outputs:
- attended: bfloat16 [8192, 128, 128], P('ctx', 'head')
- log_total: float32 [128, 8192], P('head', 'ctx')
The draws below stay inside these ranges and needn't reach their ends.
All inputs are finite; a program needn't handle non-finite values.
Results may differ from the reference program's by a relative error of at most 0.0059.
Values may be sent and summed in bfloat16 or wider, within the bound.
No kernel may reach another device: no remote copies, remote signals or barrier semaphores. Data moves between devices by JAX's collectives and lax.ppermute only.
A program may use at most 128 MiB of HBM per device.

```python
import jax
import jax.numpy as jnp
from jax import lax

HEADS = 128
LATENT = 512
ROPE = 64
NOPE = 128
VDIM = 128
TOK_DEV = 256
HOPS = 2
TOKENS = 8192
N_CTX = 32


def shared_rope(key):
    return jax.random.normal(key, (TOKENS, ROPE), jnp.float32)


def draw_latent(key, part):
    rope_part = shared_rope(key)
    key = jax.random.fold_in(key, 11)
    compressed = jax.random.normal(key, (TOKENS, LATENT), jnp.float32)
    compressed = jnp.clip(compressed, -6.0, 6.0)
    rope_part = jnp.clip(rope_part, -6.0, 6.0)
    return jnp.concatenate([compressed, rope_part], 1).astype(jnp.bfloat16)


def draw_q_rope(key, part):
    key = jax.random.fold_in(key, 23)
    first = jax.random.fold_in(key, 0)
    base = jnp.clip(jax.random.normal(first, (TOKENS, HEADS * ROPE), jnp.float32), -6.0, 6.0)
    return base.astype(jnp.bfloat16)


def steps_of(stream_key, dims, shards, low, top_value):
    level, own = 1.0, jax.random.fold_in(stream_key, 6)
    for dim, blocks in shards:
        steps = jnp.exp(jax.random.uniform(jax.random.fold_in(own, dim), (blocks,), jnp.float32, low / len(shards), top_value / len(shards)))
        level = level * jnp.repeat(steps, dims[dim] // blocks).reshape([-1 if axis == dim else 1 for axis in range(len(dims))])
    return level


def scatter_about(key, shape, width, limit, pieces=(), held_as=jnp.bfloat16):
    values = width * jax.random.normal(key, shape, jnp.float32)
    if pieces:
        values = values * steps_of(key, shape, pieces, -0.22, 0.18)
    return jnp.clip(values, -limit, limit).astype(held_as)


def setup_inputs(seed: int = 0) -> dict:
    seeds = jax.random.split(jax.random.key(seed), 7)
    return {
        "q_nope": scatter_about(seeds[0], (TOKENS, HEADS, NOPE), 1.0, 6.0, ((0, 32), (1, 8))),
        "q_rope": draw_q_rope(jax.random.fold_in(seeds[6], 71), 0),
        "latent": draw_latent(jax.random.fold_in(seeds[6], 71), 0),
        "w_uk": scatter_about(seeds[3], (LATENT, HEADS, NOPE), LATENT ** -0.5, 0.25, ((1, 8),)),
        "w_uv": scatter_about(seeds[4], (LATENT, HEADS, VDIM), LATENT ** -0.5, 0.25, ((1, 8),)),
        "span_order": jax.random.permutation(seeds[5], 2 * N_CTX).astype(jnp.int32),
    }


def reference(q_nope, q_rope, latent, w_uk, w_uv, span_order):
    cycle = N_CTX
    rows = TOK_DEV
    half = rows // 2
    compressed = latent[:, :LATENT].astype(jnp.float32)
    rope_keys = latent[:, LATENT:]
    keys_nope = jnp.einsum("tc,chd->thd", compressed, w_uk.astype(jnp.float32)).astype(jnp.bfloat16)
    values = jnp.einsum("tc,chd->thd", compressed, w_uv.astype(jnp.float32)).astype(jnp.bfloat16)
    index = jnp.arange(TOKENS, dtype=jnp.int32)
    group = index // rows
    within = index % rows
    slots = (2 * group + within // half).astype(jnp.int32)
    position = span_order[slots] * half + within % half
    offsets = [0] + list(range(1, HOPS + 1)) + [-k for k in range(1, HOPS + 1)]
    scale = 1.0 / (NOPE + ROPE) ** 0.5

    def one_group(device):
        start = (device * rows).astype(jnp.int32)
        query_a = lax.dynamic_slice_in_dim(q_nope, start, rows, 0).astype(jnp.float32)
        query_b = lax.dynamic_slice_in_dim(q_rope, start, rows, 0).astype(jnp.float32).reshape(rows, HEADS, ROPE)
        query_pos = lax.dynamic_slice_in_dim(position, start, rows, 0)
        key_list, value_list, rope_list, pos_list = [], [], [], []
        for step in offsets:
            source = (((device - step) % cycle) * rows).astype(jnp.int32)
            key_list.append(lax.dynamic_slice_in_dim(keys_nope, source, rows, 0))
            value_list.append(lax.dynamic_slice_in_dim(values, source, rows, 0))
            rope_list.append(lax.dynamic_slice_in_dim(rope_keys, source, rows, 0))
            pos_list.append(lax.dynamic_slice_in_dim(position, source, rows, 0))
        keys_a = jnp.concatenate(key_list, 0).astype(jnp.float32)
        keys_v = jnp.concatenate(value_list, 0).astype(jnp.float32)
        keys_b = jnp.concatenate(rope_list, 0).astype(jnp.float32)
        key_pos = jnp.concatenate(pos_list, 0)
        scores = jnp.einsum("qhd,khd->hqk", query_a, keys_a) + jnp.einsum("qhr,kr->hqk", query_b, keys_b)
        scores = scores * scale
        visible = (key_pos[None, :] <= query_pos[:, None])[None]
        scores = jnp.where(visible, scores, -jnp.inf)
        top = jnp.max(scores, axis=2, keepdims=True)
        expo = jnp.exp(scores - top)
        total = jnp.sum(expo, axis=2, keepdims=True)
        weights = (expo / total).astype(jnp.bfloat16)
        output = jnp.einsum("hqk,khd->qhd", weights.astype(jnp.float32), keys_v).astype(jnp.bfloat16)
        return output, (top + jnp.log(total))[:, :, 0]

    outputs, totals = lax.map(one_group, jnp.arange(cycle, dtype=jnp.int32))
    attended = outputs.reshape(TOKENS, HEADS, VDIM)
    log_total = jnp.transpose(totals, (1, 0, 2)).reshape(HEADS, TOKENS)
    return attended, log_total
```

```python
import functools
import math

import jax
import jax.numpy as jnp
from jax import lax
from jax.experimental import pallas as pl
from jax.experimental.pallas import tpu as pltpu
from jax.sharding import PartitionSpec as P

ROWS = 256
HALF = 128
HEADS = 16
NOPE = 128
ROPE = 64
LATENT = 512
PAIRS = HEADS // 2
HIDDEN = -1e30
BF = jnp.bfloat16
F32 = jnp.float32
SCALE = 1.0 / (NOPE + ROPE) ** 0.5
TO_BASE2 = SCALE * math.log2(math.e)
SLOTS = 4


def dot(a, b):
    return jnp.dot(a, b, preferred_element_type=F32)


def dot_nt(a, b):
    return lax.dot_general(a, b, (((1,), (1,)), ((), ())), preferred_element_type=F32)


def partner(kind, i, cycle):
    chip = i // 2
    if kind == "mate":
        step = 1 - 2 * (i % 2)
    elif kind == "cross":
        step = 2 * (i % 2) - 1
    elif kind == "even":
        step = 2 - 4 * (chip % 2)
    elif kind == "odd":
        step = 4 * (chip % 2) - 2
    else:
        step = 0
    return (i + step + cycle) % cycle


def exchange(block, kind):
    cycle = lax.axis_size("ctx")
    return lax.ppermute(block, "ctx", [(partner(kind, i, cycle), i) for i in range(cycle)])


def prepare_block(span_ref, me, cycle, kind, turned, lat, ext, start):
    there = partner(kind, me, cycle)
    lane = lax.broadcasted_iota(jnp.int32, (ROPE, ROWS), 1)
    row = lax.broadcasted_iota(jnp.int32, (ROPE, ROWS), 0)
    span = jnp.where(lane < HALF, span_ref[2 * there], span_ref[2 * there + 1])
    mine = jnp.where(row == 0, span_ref[2 * me], span_ref[2 * me + 1])
    bias = jnp.where((row < 2) & (span > mine), HIDDEN, 0.0).astype(BF)
    lat[start : start + ROWS] = turned[:LATENT].T
    ext[start : start + ROWS] = jnp.concatenate([turned[LATENT:], bias], 0).T


def attend(keys, own, weights_k, weights_v, queries, lat, ext, scratch, before, finish):
    k_buf, v_buf, s_buf, p_buf, m_buf = scratch
    ones = jnp.ones((keys, NOPE), BF)
    if own:
        q_at = lax.broadcasted_iota(jnp.int32, (ROWS, ROWS), 0)
        k_at = lax.broadcasted_iota(jnp.int32, (ROWS, ROWS), 1)
        later = (q_at // HALF == k_at // HALF) & (k_at > q_at)
        own_bias = jnp.where(later, HIDDEN, 0.0).astype(F32)

    def project(pair):
        k_buf[pair % SLOTS] = dot(lat[...], weights_k(pair)).astype(BF)
        v_buf[pair % SLOTS] = dot(lat[...], weights_v(pair)).astype(BF)

    def score(pair):
        for j in range(2):
            head = 2 * pair + j
            part = k_buf[pair % SLOTS, :, j * NOPE : (j + 1) * NOPE]
            scores = dot_nt(queries[head], jnp.concatenate([part, ext[...]], 1))
            if own:
                scores = scores + own_bias
            s_buf[pair % 2, j] = scores
            top = jnp.max(scores, axis=1, keepdims=True)
            if before is not None:
                top = jnp.maximum(top, before(head)[0])
            m_buf[pair % SLOTS, j] = jnp.broadcast_to(top, (ROWS, NOPE))

    def weigh(pair):
        for j in range(2):
            top = m_buf[pair % SLOTS, j][:, :1]
            p_buf[pair % 2, j] = jnp.exp2((s_buf[pair % 2, j] - top) * TO_BASE2).astype(BF)

    def combine(pair):
        for j in range(2):
            head = 2 * pair + j
            part = v_buf[pair % SLOTS, :, j * NOPE : (j + 1) * NOPE]
            both = dot(p_buf[pair % 2, j], jnp.concatenate([part, ones], 1))
            total, acc = both[:, NOPE:], both[:, :NOPE]
            top = m_buf[pair % SLOTS, j]
            if before is not None:
                top0, total0, acc0 = before(head)
                fade = jnp.exp2((top0 - top) * TO_BASE2)
                total = total + total0 * fade
                acc = acc + acc0 * fade
            finish(head, top, total, acc)

    for step in range(-2, PAIRS + 1):
        for stage, ahead in ((combine, -1), (weigh, 0), (score, 1), (project, 2)):
            if 0 <= step + ahead < PAIRS:
                stage(step + ahead)


def scratch_for(keys):
    return [
        pltpu.VMEM((keys, LATENT), BF),
        pltpu.VMEM((keys, NOPE), BF),
        pltpu.VMEM((SLOTS, keys, 2 * NOPE), BF),
        pltpu.VMEM((SLOTS, keys, 2 * NOPE), BF),
        pltpu.VMEM((2, 2, ROWS, keys), F32),
        pltpu.VMEM((2, 2, ROWS, keys), BF),
        pltpu.VMEM((SLOTS, 2, ROWS, NOPE), F32),
    ]


def first_kernel(
    span_ref, q_nope, q_rope, turned, w_uk, w_uv,
    queries, weights_k, weights_v, acc_out, stats_out,
    q_in, k_in, v_in, sems, lat, ext, *scratch,
):
    copies = [
        pltpu.make_async_copy(source, target, sems.at[i])
        for i, (source, target) in enumerate(((q_nope, q_in), (w_uk, k_in), (w_uv, v_in)))
    ]
    for copy in copies:
        copy.start()
    me = lax.axis_index("ctx")
    cycle = lax.axis_size("ctx")
    prepare_block(span_ref, me, cycle, "own", turned, lat, ext, 0)
    at = lax.broadcasted_iota(jnp.int32, (ROWS, ROPE), 1)
    row = lax.broadcasted_iota(jnp.int32, (ROWS, ROPE), 0)
    which = jnp.where(at == row // HALF, 1.0, 0.0).astype(BF)
    copies[0].wait()
    by_head = jnp.swapaxes(q_in[...], 0, 1)
    for head in range(HEADS):
        queries[head, :, :NOPE] = by_head[head]
        queries[head, :, NOPE:] = jnp.concatenate(
            [q_rope[:, head * ROPE : (head + 1) * ROPE], which], 1
        )
    for copy, source, target in ((copies[1], k_in, weights_k), (copies[2], v_in, weights_v)):
        copy.wait()
        by_head = jnp.swapaxes(source[...], 0, 1)
        for head in range(HEADS):
            target[head // 2, :, (head % 2) * NOPE : (head % 2 + 1) * NOPE] = by_head[head]
    lane = lax.broadcasted_iota(jnp.int32, (ROWS, NOPE), 1)

    def finish(head, top, total, acc):
        acc_out[head] = acc
        held = jnp.where(lane == head, top, total)
        if head == 0:
            stats_out[...] = held
        else:
            keep = (lane != head) & (lane != HEADS + head)
            stats_out[...] = jnp.where(keep, stats_out[...], held)

    attend(
        ROWS, True, lambda p: weights_k[p], lambda p: weights_v[p], queries, lat, ext,
        scratch, None, finish,
    )


def last_kernel(kinds, span_ref, *refs):
    count = len(kinds)
    turned = refs[:count]
    queries, weights_k, weights_v, acc_in, stats_in = refs[count : count + 5]
    attended, log_total, out_heads, log_cols, lat, ext, *scratch = refs[count + 5 :]
    me = lax.axis_index("ctx")
    cycle = lax.axis_size("ctx")
    for n, kind in enumerate(kinds):
        prepare_block(span_ref, me, cycle, kind, turned[n], lat, ext, n * ROWS)
    lane = lax.broadcasted_iota(jnp.int32, (ROWS, NOPE), 1)

    def before(head):
        return (
            stats_in[:, head : head + 1],
            stats_in[:, HEADS + head : HEADS + head + 1],
            acc_in[head],
        )

    def finish(head, top, total, acc):
        out_heads[head] = (acc / total).astype(BF)
        logs = top * SCALE + jnp.log(total)
        log_cols[...] = jnp.where(lane == head, logs, log_cols[...] if head else 0.0)

    attend(
        count * ROWS, False, lambda p: weights_k[p], lambda p: weights_v[p], queries, lat, ext,
        scratch, before, finish,
    )
    attended[...] = jnp.swapaxes(out_heads[...], 0, 1)
    log_total[...] = log_cols[...].T[:HEADS]


HELD = (
    ((HEADS, ROWS, 2 * NOPE), BF),
    ((PAIRS, LATENT, 2 * NOPE), BF),
    ((PAIRS, LATENT, 2 * NOPE), BF),
    ((HEADS, ROWS, NOPE), F32),
    ((ROWS, NOPE), F32),
)


def local(q_nope, q_rope, latent, w_uk, w_uv, span_order):
    turned = latent.T
    kinds = ("mate", "even", "odd", "cross")
    arrived = [exchange(turned, kind) for kind in kinds]
    smem = pl.BlockSpec(memory_space=pltpu.SMEM)
    vmem = pl.BlockSpec(memory_space=pltpu.VMEM)
    hbm = pl.BlockSpec(memory_space=pl.ANY)
    held = pl.pallas_call(
        first_kernel,
        out_shape=[pltpu.VMEM(shape, dtype) for shape, dtype in HELD],
        in_specs=[smem, hbm, vmem, vmem, hbm, hbm],
        out_specs=[vmem] * len(HELD),
        scratch_shapes=[
            pltpu.VMEM((ROWS, HEADS, NOPE), BF),
            pltpu.VMEM((LATENT, HEADS, NOPE), BF),
            pltpu.VMEM((LATENT, HEADS, NOPE), BF),
            pltpu.SemaphoreType.DMA((3,)),
        ]
        + scratch_for(ROWS),
        compiler_params=pltpu.CompilerParams(vmem_limit_bytes=20 << 20),
        cost_estimate=pl.CostEstimate(flops=int(1.7e9), bytes_accessed=15 << 20, transcendentals=1 << 20),
        name="own_block",
    )(span_order, q_nope, q_rope, turned, w_uk, w_uv)
    held = [pltpu.with_memory_space_constraint(x, pltpu.VMEM) for x in held]
    return pl.pallas_call(
        functools.partial(last_kernel, kinds),
        out_shape=[
            jax.ShapeDtypeStruct((ROWS, HEADS, NOPE), BF),
            jax.ShapeDtypeStruct((HEADS, ROWS), F32),
        ],
        in_specs=[smem] + [vmem] * (len(kinds) + len(HELD)),
        out_specs=[vmem, vmem],
        scratch_shapes=[
            pltpu.VMEM((HEADS, ROWS, NOPE), BF),
            pltpu.VMEM((ROWS, NOPE), F32),
        ]
        + scratch_for(len(kinds) * ROWS),
        compiler_params=pltpu.CompilerParams(vmem_limit_bytes=28 << 20),
        cost_estimate=pl.CostEstimate(flops=int(7e9), bytes_accessed=10 << 20, transcendentals=4 << 20),
        name="other_blocks",
    )(span_order, *arrived, *held)


def solution(mesh):
    return jax.shard_map(
        local,
        mesh=mesh,
        in_specs=(
            P("ctx", "head", None),
            P("ctx", "head"),
            P("ctx", None),
            P(None, "head", None),
            P(None, "head", None),
            P(),
        ),
        out_specs=(P("ctx", "head", None), P("head", "ctx")),
        check_vma=False,
    )
```

```python
import functools
import math

import jax
import jax.numpy as jnp
from jax import lax
from jax.experimental import pallas as pl
from jax.experimental.pallas import tpu as pltpu
from jax.sharding import PartitionSpec as P

ROWS = 256
HALF = 128
HEADS = 16
NOPE = 128
ROPE = 64
LATENT = 512
PAIRS = HEADS // 2
HIDDEN = -1e30
BF = jnp.bfloat16
F32 = jnp.float32
SCALE = 1.0 / (NOPE + ROPE) ** 0.5
TO_BASE2 = SCALE * math.log2(math.e)
SLOTS = 4
CHUNKS = 4


def dot(a, b):
    return jnp.dot(a, b, preferred_element_type=F32)


def dot_nt(a, b):
    return lax.dot_general(a, b, (((1,), (1,)), ((), ())), preferred_element_type=F32)


def partner(kind, i, cycle):
    chip = i // 2
    if kind == "mate":
        step = 1 - 2 * (i % 2)
    elif kind == "cross":
        step = 2 * (i % 2) - 1
    elif kind == "even":
        step = 2 - 4 * (chip % 2)
    elif kind == "odd":
        step = 4 * (chip % 2) - 2
    else:
        step = 0
    return (i + step + cycle) % cycle


def exchange(block, kind):
    cycle = lax.axis_size("ctx")
    return lax.ppermute(block, "ctx", [(partner(kind, i, cycle), i) for i in range(cycle)])


def visibility(span_ref, me, cycle, kind):
    there = partner(kind, me, cycle)
    lane = lax.broadcasted_iota(jnp.int32, (ROPE, ROWS), 1)
    row = lax.broadcasted_iota(jnp.int32, (ROPE, ROWS), 0)
    span = jnp.where(lane < HALF, span_ref[2 * there], span_ref[2 * there + 1])
    mine = jnp.where(row == 0, span_ref[2 * me], span_ref[2 * me + 1])
    return jnp.where((row < 2) & (span > mine), HIDDEN, 0.0).astype(BF)


def place_block(turned, bias, lat, ext, start):
    lat[start : start + ROWS] = turned[:LATENT].T
    ext[start : start + ROWS] = jnp.concatenate([turned[LATENT:], bias], 0).T


def attend(keys, own, weights_k, weights_v, queries, lat, ext, scratch, before, finish):
    k_buf, v_buf, s_buf, p_buf, m_buf = scratch
    ones = jnp.ones((keys, NOPE), BF)
    if own:
        q_at = lax.broadcasted_iota(jnp.int32, (ROWS, ROWS), 0)
        k_at = lax.broadcasted_iota(jnp.int32, (ROWS, ROWS), 1)
        later = (q_at // HALF == k_at // HALF) & (k_at > q_at)
        own_bias = jnp.where(later, HIDDEN, 0.0).astype(F32)

    def project(pair):
        k_buf[pair % SLOTS] = dot(lat[...], weights_k[pair]).astype(BF)
        v_buf[pair % SLOTS] = dot(lat[...], weights_v[pair]).astype(BF)

    def score(pair):
        for j in range(2):
            head = 2 * pair + j
            part = k_buf[pair % SLOTS, :, j * NOPE : (j + 1) * NOPE]
            scores = dot_nt(queries[head], jnp.concatenate([part, ext[...]], 1))
            if own:
                masked = scores[:, :ROWS] + own_bias
                scores = jnp.concatenate([masked, scores[:, ROWS:]], 1) if keys > ROWS else masked
            s_buf[pair % 2, j] = scores
            top = jnp.broadcast_to(jnp.max(scores, axis=1, keepdims=True), (ROWS, NOPE))
            if before is not None:
                top = jnp.maximum(top, before(head)[0])
            m_buf[pair % SLOTS, j] = top

    def weigh(pair):
        for j in range(2):
            top = m_buf[pair % SLOTS, j]
            for at in range(0, keys, NOPE):
                less = s_buf[pair % 2, j, :, at : at + NOPE] - top
                p_buf[pair % 2, j, :, at : at + NOPE] = jnp.exp2(less * TO_BASE2).astype(BF)

    def combine(pair):
        for j in range(2):
            head = 2 * pair + j
            part = v_buf[pair % SLOTS, :, j * NOPE : (j + 1) * NOPE]
            both = dot(p_buf[pair % 2, j], jnp.concatenate([part, ones], 1))
            total, acc = both[:, NOPE:], both[:, :NOPE]
            top = m_buf[pair % SLOTS, j]
            if before is not None:
                top0, total0, acc0 = before(head)
                fade = jnp.exp2((top0 - top) * TO_BASE2)
                total = total + total0 * fade
                acc = acc + acc0 * fade
            finish(head, top, total, acc)

    for step in range(-2, PAIRS + 1):
        for stage, ahead in ((project, 2), (score, 1), (weigh, 0), (combine, -1)):
            if 0 <= step + ahead < PAIRS:
                stage(step + ahead)


def attend_scratch(keys):
    return [
        pltpu.VMEM((keys, LATENT), BF),
        pltpu.VMEM((keys, NOPE), BF),
        pltpu.VMEM((SLOTS, keys, 2 * NOPE), BF),
        pltpu.VMEM((SLOTS, keys, 2 * NOPE), BF),
        pltpu.VMEM((2, 2, ROWS, keys), F32),
        pltpu.VMEM((2, 2, ROWS, keys), BF),
        pltpu.VMEM((SLOTS, 2, ROWS, NOPE), F32),
    ]


def prepare_kernel(
    spans, q_nope, q_rope, latent, w_uk, w_uv,
    queries, weights_k, weights_v, lat, ext, bias,
    span_ref, turned, q_in, r_in, k_in, v_in, sems,
):
    moves = [(spans, span_ref), (latent, turned), (q_nope, q_in), (q_rope, r_in)]
    chunk = LATENT // CHUNKS
    for source, target in ((w_uk, k_in), (w_uv, v_in)):
        for n in range(CHUNKS):
            rows = pl.ds(n * chunk, chunk)
            moves.append((source.at[rows], target.at[rows]))
    copies = [
        pltpu.make_async_copy(source, target, sems.at[i])
        for i, (source, target) in enumerate(moves)
    ]
    for copy in copies:
        copy.start()
    copies[0].wait()
    copies[1].wait()
    me = lax.axis_index("ctx")
    cycle = lax.axis_size("ctx")
    place_block(turned, visibility(span_ref, me, cycle, "own"), lat, ext, 0)
    for n, kind in enumerate(KINDS):
        bias[n] = visibility(span_ref, me, cycle, kind)
    at = lax.broadcasted_iota(jnp.int32, (ROWS, ROPE), 1)
    row = lax.broadcasted_iota(jnp.int32, (ROWS, ROPE), 0)
    which = jnp.where(at == row // HALF, 1.0, 0.0).astype(BF)
    copies[2].wait()
    copies[3].wait()
    by_head = jnp.swapaxes(q_in[...], 0, 1)
    for head in range(HEADS):
        queries[head, :, :NOPE] = by_head[head]
        queries[head, :, NOPE:] = jnp.concatenate(
            [r_in[:, head * ROPE : (head + 1) * ROPE], which], 1
        )
    for w, (source, target) in enumerate(((k_in, weights_k), (v_in, weights_v))):
        for n in range(CHUNKS):
            copies[4 + w * CHUNKS + n].wait()
            rows = slice(n * chunk, (n + 1) * chunk)
            by_head = jnp.swapaxes(source[rows], 0, 1)
            for head in range(HEADS):
                columns = slice((head % 2) * NOPE, (head % 2 + 1) * NOPE)
                target[head // 2, rows, columns] = by_head[head]


def early_kernel(kinds, queries, weights_k, weights_v, own_lat, own_ext, bias, *refs):
    count = len(kinds)
    blocks, (acc_out, top_out, total_out, lat, ext, *scratch) = refs[:count], refs[count:]
    lat[:ROWS] = own_lat[...]
    ext[:ROWS] = own_ext[...]
    for n, (kind, turned) in enumerate(zip(kinds, blocks)):
        place_block(turned, bias[KINDS.index(kind)], lat, ext, (n + 1) * ROWS)

    def finish(head, top, total, acc):
        acc_out[head] = acc
        top_out[head] = top
        total_out[head] = total

    keys = (count + 1) * ROWS
    attend(keys, True, weights_k, weights_v, queries, lat, ext, scratch, None, finish)


def late_kernel(kinds, queries, weights_k, weights_v, bias, acc_in, top_in, total_in, *refs):
    count = len(kinds)
    blocks, refs = refs[:count], refs[count:]
    attended, log_total, out_heads, tops, totals, lat, ext, *scratch = refs
    for n, (kind, turned) in enumerate(zip(kinds, blocks)):
        place_block(turned, bias[KINDS.index(kind)], lat, ext, n * ROWS)
    lane = lax.broadcasted_iota(jnp.int32, (ROWS, NOPE), 1)

    def before(head):
        return top_in[head], total_in[head], acc_in[head]

    def finish(head, top, total, acc):
        out_heads[head] = (acc / total).astype(BF)
        tops[...] = jnp.where(lane == head, top, tops[...]) if head else top
        totals[...] = jnp.where(lane == head, total, totals[...]) if head else total

    keys = count * ROWS
    attend(keys, False, weights_k, weights_v, queries, lat, ext, scratch, before, finish)
    attended[...] = jnp.swapaxes(out_heads[...], 0, 1)
    log_total[...] = (tops[...] * SCALE + jnp.log(totals[...])).T[:HEADS]


KINDS = ("mate", "even", "odd", "cross")
EARLY = ("mate", "even")
LATE = ("odd", "cross")
STATE = [pltpu.VMEM((HEADS, ROWS, NOPE), F32)] * 3
WHOLE = pl.BlockSpec(memory_space=pltpu.VMEM)
ANYWHERE = pl.BlockSpec(memory_space=pl.ANY)


def params():
    return pltpu.CompilerParams(vmem_limit_bytes=24 << 20)


def cost(blocks):
    return pl.CostEstimate(
        flops=int(1.75e9 * blocks), bytes_accessed=8 << 20, transcendentals=blocks << 20
    )


def in_hbm(*arrays):
    return [pltpu.with_memory_space_constraint(x, pltpu.HBM) for x in arrays]


def in_vmem(*arrays):
    return [pltpu.with_memory_space_constraint(x, pltpu.VMEM) for x in arrays]


def prepare(*inputs):
    outs = [
        pltpu.VMEM((HEADS, ROWS, 2 * NOPE), BF),
        pltpu.VMEM((PAIRS, LATENT, 2 * NOPE), BF),
        pltpu.VMEM((PAIRS, LATENT, 2 * NOPE), BF),
        pltpu.VMEM((ROWS, LATENT), BF),
        pltpu.VMEM((ROWS, NOPE), BF),
        pltpu.VMEM((len(KINDS), ROPE, ROWS), BF),
    ]
    return pl.pallas_call(
        prepare_kernel,
        out_shape=outs,
        in_specs=[ANYWHERE] * 6,
        out_specs=[WHOLE] * len(outs),
        scratch_shapes=[
            pltpu.SMEM((2 * lax.axis_size("ctx"),), jnp.int32),
            pltpu.VMEM((LATENT + ROPE, ROWS), BF),
            pltpu.VMEM((ROWS, HEADS, NOPE), BF),
            pltpu.VMEM((ROWS, HEADS * ROPE), BF),
            pltpu.VMEM((LATENT, HEADS, NOPE), BF),
            pltpu.VMEM((LATENT, HEADS, NOPE), BF),
            pltpu.SemaphoreType.DMA((4 + 2 * CHUNKS,)),
        ],
        compiler_params=params(),
        cost_estimate=cost(1),
        name="prepare",
    )(*in_hbm(*inputs))


def attend_early(prepared, blocks):
    return pl.pallas_call(
        functools.partial(early_kernel, EARLY),
        out_shape=STATE,
        in_specs=[WHOLE] * (len(prepared) + len(blocks)),
        out_specs=[WHOLE] * len(STATE),
        scratch_shapes=attend_scratch((len(EARLY) + 1) * ROWS),
        compiler_params=params(),
        cost_estimate=cost(len(EARLY) + 1),
        name="early_blocks",
    )(*in_vmem(*prepared, *blocks))


def attend_late(prepared, state, blocks):
    queries, weights_k, weights_v, _, _, bias = prepared
    held = (queries, weights_k, weights_v, bias, *state, *blocks)
    return pl.pallas_call(
        functools.partial(late_kernel, LATE),
        out_shape=[
            jax.ShapeDtypeStruct((ROWS, HEADS, NOPE), BF),
            jax.ShapeDtypeStruct((HEADS, ROWS), F32),
        ],
        in_specs=[WHOLE] * len(held),
        out_specs=[WHOLE] * 2,
        scratch_shapes=[
            pltpu.VMEM((HEADS, ROWS, NOPE), BF),
            pltpu.VMEM((ROWS, NOPE), F32),
            pltpu.VMEM((ROWS, NOPE), F32),
        ]
        + attend_scratch(len(LATE) * ROWS),
        compiler_params=params(),
        cost_estimate=cost(len(LATE)),
        name="late_blocks",
    )(*in_vmem(*held))


def local(q_nope, q_rope, latent, w_uk, w_uv, span_order):
    turned = latent.T
    arrived = {kind: exchange(turned, kind) for kind in KINDS}
    prepared = prepare(span_order, q_nope, q_rope, turned, w_uk, w_uv)
    state = attend_early(prepared, [arrived[kind] for kind in EARLY])
    return attend_late(prepared, state, [arrived[kind] for kind in LATE])


def solution(mesh):
    return jax.shard_map(
        local,
        mesh=mesh,
        in_specs=(
            P("ctx", "head", None),
            P("ctx", "head"),
            P("ctx", None),
            P(None, "head", None),
            P(None, "head", None),
            P(),
        ),
        out_specs=(P("ctx", "head", None), P("head", "ctx")),
        check_vma=False,
    )
```

```python
import functools
import math

import jax
import jax.numpy as jnp
from jax import lax
from jax.experimental import pallas as pl
from jax.experimental.pallas import tpu as pltpu
from jax.sharding import PartitionSpec as P

ROWS = 256
HALF = 128
HEADS = 16
NOPE = 128
ROPE = 64
LATENT = 512
PAIRS = HEADS // 2
HIDDEN = -1e30
BF = jnp.bfloat16
F32 = jnp.float32
SCALE = 1.0 / (NOPE + ROPE) ** 0.5
TO_BASE2 = SCALE * math.log2(math.e)
SLOTS = 4
CHUNKS = 4


def dot(a, b):
    return jnp.dot(a, b, preferred_element_type=F32)


def dot_nt(a, b):
    return lax.dot_general(a, b, (((1,), (1,)), ((), ())), preferred_element_type=F32)


def partner(kind, i, cycle):
    chip = i // 2
    if kind == "mate":
        step = 1 - 2 * (i % 2)
    elif kind == "cross":
        step = 2 * (i % 2) - 1
    elif kind == "even":
        step = 2 - 4 * (chip % 2)
    elif kind == "odd":
        step = 4 * (chip % 2) - 2
    else:
        step = 0
    return (i + step + cycle) % cycle


def exchange(block, kind, held_by_mate=False):
    cycle = lax.axis_size("ctx")
    pairs = [(partner(kind, i, cycle) ^ held_by_mate, i) for i in range(cycle)]
    return lax.ppermute(block, "ctx", pairs)


def visibility(span_ref, me, cycle, kind):
    there = partner(kind, me, cycle)
    lane = lax.broadcasted_iota(jnp.int32, (ROPE, ROWS), 1)
    row = lax.broadcasted_iota(jnp.int32, (ROPE, ROWS), 0)
    span = jnp.where(lane < HALF, span_ref[2 * there], span_ref[2 * there + 1])
    mine = jnp.where(row == 0, span_ref[2 * me], span_ref[2 * me + 1])
    return jnp.where((row < 2) & (span > mine), HIDDEN, 0.0).astype(BF)


def place_block(turned, bias, lat, ext, start):
    lat[start : start + ROWS] = turned[:LATENT].T
    ext[start : start + ROWS] = jnp.concatenate([turned[LATENT:], bias], 0).T


def attend(keys, own, weights_k, weights_v, queries, lat, ext, scratch, before, finish):
    k_buf, v_buf, s_buf, p_buf, m_buf = scratch
    ones = jnp.ones((keys, NOPE), BF)
    if own:
        q_at = lax.broadcasted_iota(jnp.int32, (ROWS, ROWS), 0)
        k_at = lax.broadcasted_iota(jnp.int32, (ROWS, ROWS), 1)
        later = (q_at // HALF == k_at // HALF) & (k_at > q_at)
        own_bias = jnp.where(later, HIDDEN, 0.0).astype(F32)

    def project(pair):
        k_buf[pair % SLOTS] = dot(lat[...], weights_k[pair]).astype(BF)
        v_buf[pair % SLOTS] = dot(lat[...], weights_v[pair]).astype(BF)

    def score(pair):
        for j in range(2):
            head = 2 * pair + j
            part = k_buf[pair % SLOTS, :, j * NOPE : (j + 1) * NOPE]
            scores = dot_nt(queries[head], jnp.concatenate([part, ext[...]], 1))
            if own:
                masked = scores[:, :ROWS] + own_bias
                scores = jnp.concatenate([masked, scores[:, ROWS:]], 1) if keys > ROWS else masked
            s_buf[pair % 2, j] = scores
            top = jnp.broadcast_to(jnp.max(scores, axis=1, keepdims=True), (ROWS, NOPE))
            if before is not None:
                top = jnp.maximum(top, before(head)[0])
            m_buf[pair % SLOTS, j] = top

    def weigh(pair):
        for j in range(2):
            top = m_buf[pair % SLOTS, j]
            for at in range(0, keys, NOPE):
                less = s_buf[pair % 2, j, :, at : at + NOPE] - top
                p_buf[pair % 2, j, :, at : at + NOPE] = jnp.exp2(less * TO_BASE2).astype(BF)

    def combine(pair):
        for j in range(2):
            head = 2 * pair + j
            part = v_buf[pair % SLOTS, :, j * NOPE : (j + 1) * NOPE]
            both = dot(p_buf[pair % 2, j], jnp.concatenate([part, ones], 1))
            total, acc = both[:, NOPE:], both[:, :NOPE]
            top = m_buf[pair % SLOTS, j]
            if before is not None:
                top0, total0, acc0 = before(head)
                fade = jnp.exp2((top0 - top) * TO_BASE2)
                total = total + total0 * fade
                acc = acc + acc0 * fade
            finish(head, top, total, acc)

    for step in range(-2, PAIRS + 1):
        for stage, ahead in ((project, 2), (score, 1), (weigh, 0), (combine, -1)):
            if 0 <= step + ahead < PAIRS:
                stage(step + ahead)


def attend_scratch(keys):
    return [
        pltpu.VMEM((keys, LATENT), BF),
        pltpu.VMEM((keys, NOPE), BF),
        pltpu.VMEM((SLOTS, keys, 2 * NOPE), BF),
        pltpu.VMEM((SLOTS, keys, 2 * NOPE), BF),
        pltpu.VMEM((2, 2, ROWS, keys), F32),
        pltpu.VMEM((2, 2, ROWS, keys), BF),
        pltpu.VMEM((SLOTS, 2, ROWS, NOPE), F32),
    ]


def hand_on_kernel(block, out, which):
    at = lax.broadcasted_iota(jnp.int32, (ROWS, ROPE), 1)
    row = lax.broadcasted_iota(jnp.int32, (ROWS, ROPE), 0)
    which[...] = jnp.where(at == row // HALF, 1.0, 0.0).astype(BF)


def prepare_kernel(
    spans, q_nope, q_rope, turned, w_uk, w_uv, which,
    queries, weights_k, weights_v, lat, ext, bias,
    span_ref, sem,
):
    copy = pltpu.make_async_copy(spans, span_ref, sem)
    copy.start()
    by_head = jnp.swapaxes(q_nope[...], 0, 1)
    for head in range(HEADS):
        queries[head, :, :NOPE] = by_head[head]
        queries[head, :, NOPE:] = jnp.concatenate(
            [q_rope[:, head * ROPE : (head + 1) * ROPE], which[...]], 1
        )
    for source, target in ((w_uk, weights_k), (w_uv, weights_v)):
        by_head = jnp.swapaxes(source[...], 0, 1)
        for head in range(HEADS):
            columns = slice((head % 2) * NOPE, (head % 2 + 1) * NOPE)
            target[head // 2, :, columns] = by_head[head]
    copy.wait()
    me = lax.axis_index("ctx")
    cycle = lax.axis_size("ctx")
    place_block(turned, visibility(span_ref, me, cycle, "own"), lat, ext, 0)
    for n, kind in enumerate(KINDS):
        bias[n] = visibility(span_ref, me, cycle, kind)


def early_kernel(kinds, queries, weights_k, weights_v, own_lat, own_ext, bias, *refs):
    count = len(kinds)
    blocks, (acc_out, top_out, total_out, lat, ext, *scratch) = refs[:count], refs[count:]
    lat[:ROWS] = own_lat[...]
    ext[:ROWS] = own_ext[...]
    for n, (kind, turned) in enumerate(zip(kinds, blocks)):
        place_block(turned, bias[KINDS.index(kind)], lat, ext, (n + 1) * ROWS)

    def finish(head, top, total, acc):
        acc_out[head] = acc
        top_out[head] = top
        total_out[head] = total

    keys = (count + 1) * ROWS
    attend(keys, True, weights_k, weights_v, queries, lat, ext, scratch, None, finish)


def late_kernel(kinds, queries, weights_k, weights_v, bias, acc_in, top_in, total_in, *refs):
    count = len(kinds)
    blocks, refs = refs[:count], refs[count:]
    attended, log_total, out_heads, tops, totals, lat, ext, *scratch = refs
    for n, (kind, turned) in enumerate(zip(kinds, blocks)):
        place_block(turned, bias[KINDS.index(kind)], lat, ext, n * ROWS)
    lane = lax.broadcasted_iota(jnp.int32, (ROWS, NOPE), 1)

    def before(head):
        return top_in[head], total_in[head], acc_in[head]

    def finish(head, top, total, acc):
        out_heads[head] = (acc / total).astype(BF)
        tops[...] = jnp.where(lane == head, top, tops[...]) if head else top
        totals[...] = jnp.where(lane == head, total, totals[...]) if head else total

    keys = count * ROWS
    attend(keys, False, weights_k, weights_v, queries, lat, ext, scratch, before, finish)
    attended[...] = jnp.swapaxes(out_heads[...], 0, 1)
    log_total[...] = (tops[...] * SCALE + jnp.log(totals[...])).T[:HEADS]


KINDS = ("mate", "even", "odd", "cross")
EARLY = ("mate", "even")
LATE = ("cross", "odd")
STATE = [pltpu.VMEM((HEADS, ROWS, NOPE), F32)] * 3
WHOLE = pl.BlockSpec(memory_space=pltpu.VMEM)
ANYWHERE = pl.BlockSpec(memory_space=pl.ANY)


def params():
    return pltpu.CompilerParams(vmem_limit_bytes=24 << 20)


def cost(blocks):
    return pl.CostEstimate(
        flops=int(1.75e9 * blocks), bytes_accessed=8 << 20, transcendentals=blocks << 20
    )


def in_hbm(*arrays):
    return [pltpu.with_memory_space_constraint(x, pltpu.HBM) for x in arrays]


def in_vmem(*arrays):
    return [pltpu.with_memory_space_constraint(x, pltpu.VMEM) for x in arrays]


def prepare(spans, *inputs):
    outs = [
        pltpu.VMEM((HEADS, ROWS, 2 * NOPE), BF),
        pltpu.VMEM((PAIRS, LATENT, 2 * NOPE), BF),
        pltpu.VMEM((PAIRS, LATENT, 2 * NOPE), BF),
        pltpu.VMEM((ROWS, LATENT), BF),
        pltpu.VMEM((ROWS, NOPE), BF),
        pltpu.VMEM((len(KINDS), ROPE, ROWS), BF),
    ]
    return pl.pallas_call(
        prepare_kernel,
        out_shape=outs,
        in_specs=[ANYWHERE] + [WHOLE] * 6,
        out_specs=[WHOLE] * len(outs),
        scratch_shapes=[
            pltpu.SMEM((2 * lax.axis_size("ctx"),), jnp.int32),
            pltpu.SemaphoreType.DMA,
        ],
        compiler_params=params(),
        cost_estimate=cost(1),
        name="prepare",
    )(*in_hbm(spans), *in_vmem(*inputs))


def hand_on(block):
    return pl.pallas_call(
        hand_on_kernel,
        out_shape=[pltpu.VMEM((LATENT + ROPE, ROWS), BF), pltpu.VMEM((ROWS, ROPE), BF)],
        in_specs=[WHOLE],
        out_specs=[WHOLE] * 2,
        input_output_aliases={0: 0},
        compiler_params=pltpu.CompilerParams(vmem_limit_bytes=4 << 20),
        cost_estimate=cost(8),
        name="hand_on",
    )(*in_vmem(block))


def attend_early(prepared, blocks):
    return pl.pallas_call(
        functools.partial(early_kernel, EARLY),
        out_shape=STATE,
        in_specs=[WHOLE] * (len(prepared) + len(blocks)),
        out_specs=[WHOLE] * len(STATE),
        scratch_shapes=attend_scratch((len(EARLY) + 1) * ROWS),
        compiler_params=params(),
        cost_estimate=cost(len(EARLY) + 1),
        name="early_blocks",
    )(*in_vmem(*prepared, *blocks))


def attend_late(prepared, state, blocks):
    queries, weights_k, weights_v, _, _, bias = prepared
    held = (queries, weights_k, weights_v, bias, *state, *blocks)
    return pl.pallas_call(
        functools.partial(late_kernel, LATE),
        out_shape=[
            jax.ShapeDtypeStruct((ROWS, HEADS, NOPE), BF),
            jax.ShapeDtypeStruct((HEADS, ROWS), F32),
        ],
        in_specs=[WHOLE] * len(held),
        out_specs=[WHOLE] * 2,
        scratch_shapes=[
            pltpu.VMEM((HEADS, ROWS, NOPE), BF),
            pltpu.VMEM((ROWS, NOPE), F32),
            pltpu.VMEM((ROWS, NOPE), F32),
        ]
        + attend_scratch(len(LATE) * ROWS),
        compiler_params=params(),
        cost_estimate=cost(len(LATE)),
        name="late_blocks",
    )(*in_vmem(*held))


def local(q_nope, q_rope, latent, w_uk, w_uv, span_order):
    turned = latent.T
    arrived = {kind: exchange(turned, kind) for kind in EARLY}
    arrived["mate"], which = hand_on(arrived["mate"])
    arrived |= {kind: exchange(arrived["mate"], kind, held_by_mate=True) for kind in LATE}
    prepared = prepare(span_order, q_nope, q_rope, turned, w_uk, w_uv, which)
    state = attend_early(prepared, [arrived[kind] for kind in EARLY])
    return attend_late(prepared, state, [arrived[kind] for kind in LATE])


def solution(mesh):
    return jax.shard_map(
        local,
        mesh=mesh,
        in_specs=(
            P("ctx", "head", None),
            P("ctx", "head"),
            P("ctx", None),
            P(None, "head", None),
            P(None, "head", None),
            P(),
        ),
        out_specs=(P("ctx", "head", None), P("head", "ctx")),
        check_vma=False,
    )
```

```python
import functools
import math

import jax
import jax.numpy as jnp
from jax import lax
from jax.experimental import pallas as pl
from jax.experimental.pallas import tpu as pltpu
from jax.sharding import PartitionSpec as P

ROWS = 256
HALF = 128
HEADS = 16
NOPE = 128
ROPE = 64
LATENT = 512
PAIRS = HEADS // 2
HIDDEN = -1e30
BF = jnp.bfloat16
F32 = jnp.float32
SCALE = 1.0 / (NOPE + ROPE) ** 0.5
TO_BASE2 = SCALE * math.log2(math.e)
SLOTS = 4
CHUNKS = 4


def dot(a, b):
    return jnp.dot(a, b, preferred_element_type=F32)


def dot_nt(a, b):
    return lax.dot_general(a, b, (((1,), (1,)), ((), ())), preferred_element_type=F32)


def partner(kind, i, cycle):
    chip = i // 2
    if kind == "mate":
        step = 1 - 2 * (i % 2)
    elif kind == "cross":
        step = 2 * (i % 2) - 1
    elif kind == "even":
        step = 2 - 4 * (chip % 2)
    elif kind == "odd":
        step = 4 * (chip % 2) - 2
    else:
        step = 0
    return (i + step + cycle) % cycle


def exchange(block, kind):
    cycle = lax.axis_size("ctx")
    return lax.ppermute(block, "ctx", [(partner(kind, i, cycle), i) for i in range(cycle)])


def visibility(span_ref, me, cycle, kind):
    there = partner(kind, me, cycle)
    lane = lax.broadcasted_iota(jnp.int32, (ROPE, ROWS), 1)
    row = lax.broadcasted_iota(jnp.int32, (ROPE, ROWS), 0)
    span = jnp.where(lane < HALF, span_ref[2 * there], span_ref[2 * there + 1])
    mine = jnp.where(row == 0, span_ref[2 * me], span_ref[2 * me + 1])
    return jnp.where((row < 2) & (span > mine), HIDDEN, 0.0).astype(BF)


def place_block(turned, bias, lat, ext, start):
    lat[start : start + ROWS] = turned[:LATENT].T
    ext[start : start + ROWS] = jnp.concatenate([turned[LATENT:], bias], 0).T


def attend(keys, own, weights_k, weights_v, queries, lat, ext, scratch, before, finish):
    k_buf, v_buf, s_buf, p_buf, m_buf = scratch
    ones = jnp.ones((keys, NOPE), BF)
    if own:
        q_at = lax.broadcasted_iota(jnp.int32, (ROWS, ROWS), 0)
        k_at = lax.broadcasted_iota(jnp.int32, (ROWS, ROWS), 1)
        later = (q_at // HALF == k_at // HALF) & (k_at > q_at)
        own_bias = jnp.where(later, HIDDEN, 0.0).astype(F32)

    def project(pair):
        k_buf[pair % SLOTS] = dot(lat[...], weights_k[pair]).astype(BF)
        v_buf[pair % SLOTS] = dot(lat[...], weights_v[pair]).astype(BF)

    def score(pair):
        for j in range(2):
            head = 2 * pair + j
            part = k_buf[pair % SLOTS, :, j * NOPE : (j + 1) * NOPE]
            scores = dot_nt(queries[head], jnp.concatenate([part, ext[...]], 1))
            if own:
                masked = scores[:, :ROWS] + own_bias
                scores = jnp.concatenate([masked, scores[:, ROWS:]], 1) if keys > ROWS else masked
            s_buf[pair % 2, j] = scores
            top = jnp.broadcast_to(jnp.max(scores, axis=1, keepdims=True), (ROWS, NOPE))
            if before is not None:
                top = jnp.maximum(top, before(head)[0])
            m_buf[pair % SLOTS, j] = top

    def weigh(pair):
        for j in range(2):
            top = m_buf[pair % SLOTS, j]
            for at in range(0, keys, NOPE):
                less = s_buf[pair % 2, j, :, at : at + NOPE] - top
                p_buf[pair % 2, j, :, at : at + NOPE] = jnp.exp2(less * TO_BASE2).astype(BF)

    def combine(pair):
        for j in range(2):
            head = 2 * pair + j
            part = v_buf[pair % SLOTS, :, j * NOPE : (j + 1) * NOPE]
            both = dot(p_buf[pair % 2, j], jnp.concatenate([part, ones], 1))
            total, acc = both[:, NOPE:], both[:, :NOPE]
            top = m_buf[pair % SLOTS, j]
            if before is not None:
                top0, total0, acc0 = before(head)
                fade = jnp.exp2((top0 - top) * TO_BASE2)
                total = total + total0 * fade
                acc = acc + acc0 * fade
            finish(head, top, total, acc)

    for step in range(-2, PAIRS + 1):
        for stage, ahead in ((project, 2), (score, 1), (weigh, 0), (combine, -1)):
            if 0 <= step + ahead < PAIRS:
                stage(step + ahead)


def attend_scratch(keys):
    return [
        pltpu.VMEM((keys, LATENT), BF),
        pltpu.VMEM((keys, NOPE), BF),
        pltpu.VMEM((SLOTS, keys, 2 * NOPE), BF),
        pltpu.VMEM((SLOTS, keys, 2 * NOPE), BF),
        pltpu.VMEM((2, 2, ROWS, keys), F32),
        pltpu.VMEM((2, 2, ROWS, keys), BF),
        pltpu.VMEM((SLOTS, 2, ROWS, NOPE), F32),
    ]


def mark_kernel(which):
    at = lax.broadcasted_iota(jnp.int32, (ROWS, ROPE), 1)
    row = lax.broadcasted_iota(jnp.int32, (ROWS, ROPE), 0)
    which[...] = jnp.where(at == row // HALF, 1.0, 0.0).astype(BF)


def prepare_kernel(
    spans, q_nope, q_rope, turned, w_uk, w_uv, which,
    queries, weights_k, weights_v, lat, ext, bias,
    span_ref, sem,
):
    copy = pltpu.make_async_copy(spans, span_ref, sem)
    copy.start()
    by_head = jnp.swapaxes(q_nope[...], 0, 1)
    for head in range(HEADS):
        queries[head, :, :NOPE] = by_head[head]
        queries[head, :, NOPE:] = jnp.concatenate(
            [q_rope[:, head * ROPE : (head + 1) * ROPE], which[...]], 1
        )
    for source, target in ((w_uk, weights_k), (w_uv, weights_v)):
        by_head = jnp.swapaxes(source[...], 0, 1)
        for head in range(HEADS):
            columns = slice((head % 2) * NOPE, (head % 2 + 1) * NOPE)
            target[head // 2, :, columns] = by_head[head]
    copy.wait()
    me = lax.axis_index("ctx")
    cycle = lax.axis_size("ctx")
    place_block(turned, visibility(span_ref, me, cycle, "own"), lat, ext, 0)
    for n, kind in enumerate(KINDS):
        bias[n] = visibility(span_ref, me, cycle, kind)


def early_kernel(kinds, queries, weights_k, weights_v, own_lat, own_ext, bias, *refs):
    count = len(kinds)
    blocks, (acc_out, top_out, total_out, lat, ext, *scratch) = refs[:count], refs[count:]
    lat[:ROWS] = own_lat[...]
    ext[:ROWS] = own_ext[...]
    for n, (kind, turned) in enumerate(zip(kinds, blocks)):
        place_block(turned, bias[KINDS.index(kind)], lat, ext, (n + 1) * ROWS)

    def finish(head, top, total, acc):
        acc_out[head] = acc
        top_out[head] = top
        total_out[head] = total

    keys = (count + 1) * ROWS
    attend(keys, True, weights_k, weights_v, queries, lat, ext, scratch, None, finish)


def late_kernel(kinds, *refs):
    count = len(kinds)
    blocks, refs = refs[:count], refs[count:]
    queries, weights_k, weights_v, bias, acc_in, top_in, total_in, *refs = refs
    attended, log_total, out_heads, tops, totals, lat, ext, *scratch = refs
    for n, (kind, turned) in enumerate(zip(kinds, blocks)):
        place_block(turned, bias[KINDS.index(kind)], lat, ext, n * ROWS)
    lane = lax.broadcasted_iota(jnp.int32, (ROWS, NOPE), 1)

    def before(head):
        return top_in[head], total_in[head], acc_in[head]

    def finish(head, top, total, acc):
        out_heads[head] = (acc / total).astype(BF)
        tops[...] = jnp.where(lane == head, top, tops[...]) if head else top
        totals[...] = jnp.where(lane == head, total, totals[...]) if head else total

    keys = count * ROWS
    attend(keys, False, weights_k, weights_v, queries, lat, ext, scratch, before, finish)
    attended[...] = jnp.swapaxes(out_heads[...], 0, 1)
    log_total[...] = (tops[...] * SCALE + jnp.log(totals[...])).T[:HEADS]


KINDS = ("mate", "even", "odd", "cross")
EARLY = ("mate", "even")
LATE = ("odd", "cross")
STATE = [pltpu.VMEM((HEADS, ROWS, NOPE), F32)] * 3
WHOLE = pl.BlockSpec(memory_space=pltpu.VMEM)
ANYWHERE = pl.BlockSpec(memory_space=pl.ANY)


def params():
    return pltpu.CompilerParams(vmem_limit_bytes=24 << 20)


def cost(blocks):
    return pl.CostEstimate(
        flops=int(1.75e9 * blocks), bytes_accessed=8 << 20, transcendentals=blocks << 20
    )


def in_hbm(*arrays):
    return [pltpu.with_memory_space_constraint(x, pltpu.HBM) for x in arrays]


def in_vmem(*arrays):
    return [pltpu.with_memory_space_constraint(x, pltpu.VMEM) for x in arrays]


def prepare(spans, *inputs):
    outs = [
        pltpu.VMEM((HEADS, ROWS, 2 * NOPE), BF),
        pltpu.VMEM((PAIRS, LATENT, 2 * NOPE), BF),
        pltpu.VMEM((PAIRS, LATENT, 2 * NOPE), BF),
        pltpu.VMEM((ROWS, LATENT), BF),
        pltpu.VMEM((ROWS, NOPE), BF),
        pltpu.VMEM((len(KINDS), ROPE, ROWS), BF),
    ]
    return pl.pallas_call(
        prepare_kernel,
        out_shape=outs,
        in_specs=[ANYWHERE] + [WHOLE] * 6,
        out_specs=[WHOLE] * len(outs),
        scratch_shapes=[
            pltpu.SMEM((2 * lax.axis_size("ctx"),), jnp.int32),
            pltpu.SemaphoreType.DMA,
        ],
        compiler_params=params(),
        cost_estimate=cost(1),
        name="prepare",
    )(*in_hbm(spans), *in_vmem(*inputs))


def mark_slots():
    return pl.pallas_call(
        mark_kernel,
        out_shape=pltpu.VMEM((ROWS, ROPE), BF),
        out_specs=WHOLE,
        compiler_params=pltpu.CompilerParams(vmem_limit_bytes=4 << 20),
        cost_estimate=cost(8),
        name="mark_slots",
    )()


def attend_early(prepared, blocks):
    return pl.pallas_call(
        functools.partial(early_kernel, EARLY),
        out_shape=STATE,
        in_specs=[WHOLE] * (len(prepared) + len(blocks)),
        out_specs=[WHOLE] * len(STATE),
        scratch_shapes=attend_scratch((len(EARLY) + 1) * ROWS),
        compiler_params=params(),
        cost_estimate=cost(len(EARLY) + 1),
        name="early_blocks",
    )(*in_vmem(*prepared, *blocks))


def attend_late(prepared, state, blocks):
    queries, weights_k, weights_v, _, _, bias = prepared
    held = (*blocks, queries, weights_k, weights_v, bias, *state)
    return pl.pallas_call(
        functools.partial(late_kernel, LATE),
        out_shape=[
            jax.ShapeDtypeStruct((ROWS, HEADS, NOPE), BF),
            jax.ShapeDtypeStruct((HEADS, ROWS), F32),
        ],
        in_specs=[WHOLE] * len(held),
        out_specs=[WHOLE] * 2,
        scratch_shapes=[
            pltpu.VMEM((HEADS, ROWS, NOPE), BF),
            pltpu.VMEM((ROWS, NOPE), F32),
            pltpu.VMEM((ROWS, NOPE), F32),
        ]
        + attend_scratch(len(LATE) * ROWS),
        compiler_params=params(),
        cost_estimate=cost(len(LATE)),
        name="late_blocks",
    )(*in_vmem(*held))


def local(q_nope, q_rope, latent, w_uk, w_uv, span_order):
    turned = latent.T
    arrived = {kind: exchange(turned, kind) for kind in KINDS}
    which = mark_slots()
    prepared = prepare(span_order, q_nope, q_rope, turned, w_uk, w_uv, which)
    state = attend_early(prepared, [arrived[kind] for kind in EARLY])
    return attend_late(prepared, state, [arrived[kind] for kind in LATE])


def solution(mesh):
    return jax.shard_map(
        local,
        mesh=mesh,
        in_specs=(
            P("ctx", "head", None),
            P("ctx", "head"),
            P("ctx", None),
            P(None, "head", None),
            P(None, "head", None),
            P(),
        ),
        out_specs=(P("ctx", "head", None), P("head", "ctx")),
        check_vma=False,
    )
```
